256 devices in a mesh: pipe: 8 (over x, core), neuron: 32 (over y, z).
Axes of the slice: x: 4, y: 4, z: 8, core: 2. Of those that a mesh axis runs over, the one named last changes fastest.
Arguments:
- inputs: bfloat16 [2, 128, 65536], P(None, None, 'neuron'), may hold values from -6 to 6
- weights: bfloat16 [8, 512, 16, 128, 128], P('pipe', 'neuron'), may hold values from -0.1875 to 0.1875
- pattern: int32 [8, 512, 16], P('pipe', 'neuron'), may hold values from 0 to 511, as said below
- bias: float32 [8, 65536], P('pipe', 'neuron'), may hold values from -1.5 to 1.5
Outputs:
- activations: bfloat16 [8, 2, 128, 65536], P('pipe', None, None, 'neuron')
The draws below stay inside these ranges and needn't reach their ends.
Inputs may be any that keep to these rules, and one draw needn't show every extreme that they name: `pattern`: entry [l, j, k] names an input block that lies in the group of 16 blocks holding output block j (groups j // 16), or in one of the two groups beside it, counted cyclically over the 32 groups; entries of one row may repeat.
All inputs are finite; a program needn't handle non-finite values.
Results may differ from the reference program's by a relative error of at most 0.015.
Values may be sent and summed in bfloat16 or wider, within the bound.
A program may use at most 128 MiB of HBM per device.

```python
import jax
import jax.numpy as jnp
from jax import lax

BS = 128
KB = 16
BLK_DEV = 16
ROWS = 128
MICRO = 2
NB = 512
NEURONS = 65536
LAYERS = 8


def draw_pattern(key, part):
    key = jax.random.fold_in(key, 11)
    key_side, key_block = jax.random.split(key)
    shape = (LAYERS, NB, KB)
    side = jax.random.randint(key_side, shape, -1, 2)
    within = jax.random.randint(key_block, shape, 0, BLK_DEV)
    group_count = NB // BLK_DEV
    owner = (jnp.arange(NB, dtype=jnp.int32) // BLK_DEV)[None, :, None]
    target = jnp.mod(owner + side, group_count)
    return (target * BLK_DEV + within).astype(jnp.int32)


def block_scale(rng, extent, cuts, low, largest):
    factor_of, own = 1.0, jax.random.fold_in(rng, 6)
    for axis_at, shards_of in cuts:
        steps = jnp.exp(jax.random.uniform(jax.random.fold_in(own, axis_at), (shards_of,), jnp.float32, low / len(cuts), largest / len(cuts)))
        factor_of = factor_of * jnp.repeat(steps, extent[axis_at] // shards_of).reshape([-1 if axis == axis_at else 1 for axis in range(len(extent))])
    return factor_of


def gaussian(rng, shape, spread, most, pieces=(), kind=jnp.bfloat16):
    result = spread * jax.random.normal(rng, shape, jnp.float32)
    if pieces:
        result = result * block_scale(rng, shape, pieces, -0.22, 0.18)
    return jnp.clip(result, -most, most).astype(kind)


def setup_inputs(seed: int = 0) -> dict:
    seeds = jax.random.split(jax.random.key(seed), 5)
    return {
        "inputs": gaussian(seeds[0], (MICRO, ROWS, NEURONS), 1.0, 6.0, ((2, 32),)),
        "weights": gaussian(seeds[1], (LAYERS, NB, KB, BS, BS), (KB * BS // 2) ** -0.5, 0.1875, ((0, 8), (1, 32))),
        "pattern": draw_pattern(jax.random.fold_in(seeds[4], 71), 0),
        "bias": gaussian(seeds[3], (LAYERS, NEURONS), 0.3, 1.5, ((0, 8), (1, 32)), jnp.float32),
    }


def reference(inputs, weights, pattern, bias):
    flat_rows = MICRO * ROWS
    current = inputs.reshape(flat_rows, NB, BS)
    results = []
    for layer in range(LAYERS):
        index_groups = pattern[layer].reshape(NB // BLK_DEV, BLK_DEV * KB)
        weight_groups = weights[layer].reshape(NB // BLK_DEV, BLK_DEV, KB, BS, BS)

        def block_group(operands, current=current):
            indices, wpart = operands
            picked = jnp.take(current, indices, axis=1).reshape(flat_rows, BLK_DEV, KB, BS)
            return jnp.einsum("rjkc,jkcd->rjd", picked.astype(jnp.float32), wpart.astype(jnp.float32))

        summed = lax.map(block_group, (index_groups, weight_groups))
        summed = jnp.transpose(summed, (1, 0, 2, 3)).reshape(flat_rows, NEURONS)
        output = jnp.maximum(summed + bias[layer], 0.0).astype(jnp.bfloat16)
        results.append(output.reshape(MICRO, ROWS, NEURONS))
        current = output.reshape(flat_rows, NB, BS)
    return jnp.stack(results)
```

```python
import functools

import jax
import jax.numpy as jnp
from jax import lax
from jax.experimental import pallas as pl
from jax.experimental.pallas import tpu as pltpu
from jax.sharding import PartitionSpec as P

MESH = pl.DeviceIdType.MESH
CHUNK = 16
PIECES = 1
DIRECT_HEAD = 0
DIRECT_TAIL = 0
DIRECT_EDGE = 0
FIRST_AHEAD = 6
EVEN_AHEAD = 3
PASS_AT = 0


def kernel(
    sections, groups, chunks, rows, blocks, entries, width, pieces,
    pattern_ref, bias_ref, x_ref, w_ref, out_ref,
    ids, landing, work, held, result,
    w_sem, in_sem, own_sem, side_sem, pass_sem, send_sem, out_sem,
):
    section = lax.axis_index("pipe")
    group = lax.axis_index("neuron")
    right = lax.rem(group + 1, groups)
    left = lax.rem(group + groups - 1, groups)
    even = lax.rem(section, 2) == 0
    first = section == 0
    later_even = jnp.logical_and(even, section > 0)
    odd = jnp.logical_not(even)
    odd_sends = jnp.logical_and(odd, section < sections - 1)
    per_piece = blocks // pieces
    span = per_piece * width

    def signal(barrier, to_section, to_group):
        pl.semaphore_signal(
            barrier, inc=1, device_id={"pipe": to_section, "neuron": to_group}, device_id_type=MESH
        )

    def weight_copy(j):
        return pltpu.make_async_copy(w_ref.at[j], held.at[j], w_sem.at[j])

    for j in range(blocks):
        weight_copy(j).start()

    beside = (group, left, right)
    any_direct = DIRECT_HEAD + DIRECT_TAIL + DIRECT_EDGE > 0

    barrier = pltpu.get_barrier_semaphore()

    @pl.when(even)
    def _():
        signal(barrier, section, left)
        signal(barrier, section, right)
        for to in beside:
            signal(barrier, section + 1, to)

    @pl.when(later_even)
    def _():
        for to in beside if any_direct else (group,):
            signal(barrier, section - 1, to)

    @pl.when(odd)
    def _():
        for to in beside:
            signal(barrier, section - 1, to)

    @pl.when(odd_sends)
    def _():
        for to in beside if any_direct else (group,):
            signal(barrier, section + 1, to)

    base = (group - 1) * blocks
    total = groups * blocks

    @pl.loop(0, blocks)
    def _(j):
        for k in range(entries):
            near = lax.rem(pattern_ref[j, k] - base + total, total)
            ids[j, k] = jnp.minimum(near, 3 * blocks - 1)

    @pl.when(first)
    def _():
        pl.semaphore_wait(barrier, 5)

    @pl.when(later_even)
    def _():
        pl.semaphore_wait(barrier, 8 if any_direct else 6)

    @pl.when(odd_sends)
    def _():
        pl.semaphore_wait(barrier, 6 if any_direct else 4)

    @pl.when(jnp.logical_and(odd, section == sections - 1))
    def _():
        pl.semaphore_wait(barrier, 3)

    def row_range(c):
        return pl.ds(pl.multiple_of(c * rows, rows), rows)

    def cols(p):
        return pl.ds(p * span, span)

    def load_copy(c):
        return pltpu.make_async_copy(x_ref.at[row_range(c)], landing.at[c, 1], in_sem.at[c])

    def remote(src, dst, send, recv, to_section, to_group):
        return pltpu.make_async_remote_copy(
            src_ref=src, dst_ref=dst, send_sem=send, recv_sem=recv,
            device_id={"pipe": to_section, "neuron": to_group}, device_id_type=MESH,
        )

    def pass_copy(c, p, side):
        return remote(
            landing.at[c, 1, :, cols(p)], landing.at[c, 2 * side, :, cols(p)],
            pass_sem.at[c, p, side], side_sem.at[c, p, side], section, (right, left)[side],
        )

    def down_copy(c, p):
        return remote(
            result.at[c, :, cols(p)], landing.at[c, 1, :, cols(p)],
            send_sem.at[c, p, 2], own_sem.at[c, p], section + 1, group,
        )

    def down_side_copy(c, p, side):
        return remote(
            result.at[c, :, cols(p)], landing.at[c, 2 * side, :, cols(p)],
            send_sem.at[c, p, side], side_sem.at[c, p, side], section + 1, (right, left)[side],
        )

    def out_copy(c):
        return pltpu.make_async_copy(result.at[c], out_ref.at[row_range(c)], out_sem.at[c])

    def goes_direct(c, side):
        yes = jnp.logical_or(c < DIRECT_HEAD, c >= chunks - DIRECT_TAIL)
        if DIRECT_EDGE:
            border = (group, left)[side]
            yes = jnp.logical_or(yes, lax.rem(border, DIRECT_EDGE) == DIRECT_EDGE - 1)
        return yes

    def passes(c, side):
        return jnp.logical_not(goes_direct(c, side))

    def sends_side(c, side):
        return jnp.logical_or(even, jnp.logical_and(odd_sends, goes_direct(c, side)))

    def pass_first(c):
        load_copy(c).wait()
        for p in range(pieces):
            for side in range(2):
                pass_copy(c, p, side).start()

    def pass_even(c):
        @pl.when(jnp.logical_and(c >= DIRECT_HEAD, c < chunks - DIRECT_TAIL))
        def _():
            for p in range(pieces):
                down_copy(c, p).wait_recv()
                for side in range(2):
                    @pl.when(passes(c, side))
                    def _():
                        pass_copy(c, p, side).start()

    def pass_on(c):
        @pl.when(jnp.logical_and(first, c + FIRST_AHEAD < chunks))
        def _():
            pass_first(c + FIRST_AHEAD)

        @pl.when(jnp.logical_and(later_even, c + EVEN_AHEAD < chunks))
        def _():
            pass_even(c + EVEN_AHEAD)

    @pl.when(first)
    def _():
        for c in range(chunks):
            load_copy(c).start()
        for c in range(FIRST_AHEAD):
            pass_first(c)

    @pl.when(later_even)
    def _():
        for c in range(EVEN_AHEAD):
            pass_even(c)

    @pl.loop(0, chunks)
    def _(c):
        if PASS_AT == 0:
            pass_on(c)

        whole = jnp.logical_or(c < DIRECT_HEAD, c >= chunks - DIRECT_TAIL)

        @pl.when(jnp.logical_or(odd, jnp.logical_and(later_even, whole)))
        def _():
            for p in range(pieces):
                down_copy(c, p).wait_recv()

        for p in range(pieces):
            for side in range(2):
                pass_copy(c, p, side).wait_recv()

        @pl.when(c == 0)
        def _():
            for j in range(blocks):
                weight_copy(j).wait()

        for side in range(3):
            for b in range(blocks):
                work[side * blocks + b] = landing[c, side, :, b * width : (b + 1) * width]

        for p in range(pieces):
            for j in range(p * per_piece, (p + 1) * per_piece):
                picked = jnp.concatenate([work[ids[j, k]] for k in range(entries)], axis=1)
                summed = jnp.dot(
                    picked, held[j].reshape(entries * width, width), preferred_element_type=jnp.float32
                )
                summed = summed + bias_ref[:, j * width : (j + 1) * width]
                result[c, :, j * width : (j + 1) * width] = jnp.maximum(summed, 0.0).astype(jnp.bfloat16)

            @pl.when(section < sections - 1)
            def _():
                down_copy(c, p).start()

            for side in range(2):
                @pl.when(sends_side(c, side))
                def _():
                    down_side_copy(c, p, side).start()

            if PASS_AT == p + 1:
                pass_on(c)

        out_copy(c).start()

    @pl.loop(0, chunks)
    def _(c):
        out_copy(c).wait()
        for p in range(pieces):
            for side in range(2):
                @pl.when(jnp.logical_or(first, jnp.logical_and(later_even, passes(c, side))))
                def _():
                    pass_copy(c, p, side).wait_send()

                @pl.when(sends_side(c, side))
                def _():
                    down_side_copy(c, p, side).wait_send()

            @pl.when(section < sections - 1)
            def _():
                down_copy(c, p).wait_send()


def per_device(sections, groups, inputs, weights, pattern, bias):
    micro, batch, columns = inputs.shape
    blocks, entries, width = weights.shape[1:4]
    rows = CHUNK
    chunks = micro * batch // rows
    out = pl.pallas_call(
        functools.partial(
            kernel, sections, groups, chunks, rows, blocks, entries, width, PIECES
        ),
        out_shape=jax.ShapeDtypeStruct((micro * batch, columns), jnp.bfloat16),
        in_specs=[
            pl.BlockSpec(memory_space=pltpu.SMEM),
            pl.BlockSpec(memory_space=pltpu.VMEM),
            pl.BlockSpec(memory_space=pl.ANY),
            pl.BlockSpec(memory_space=pl.ANY),
        ],
        out_specs=pl.BlockSpec(memory_space=pl.ANY),
        scratch_shapes=[
            pltpu.SMEM((blocks, entries), jnp.int32),
            pltpu.VMEM((chunks, 3, rows, columns), jnp.bfloat16),
            pltpu.VMEM((3 * blocks, rows, width), jnp.bfloat16),
            pltpu.VMEM((blocks, entries, width, width), jnp.bfloat16),
            pltpu.VMEM((chunks, rows, columns), jnp.bfloat16),
            pltpu.SemaphoreType.DMA((blocks,)),
            pltpu.SemaphoreType.DMA((chunks,)),
            pltpu.SemaphoreType.DMA((chunks, PIECES)),
            pltpu.SemaphoreType.DMA((chunks, PIECES, 2)),
            pltpu.SemaphoreType.DMA((chunks, PIECES, 2)),
            pltpu.SemaphoreType.DMA((chunks, PIECES, 3)),
            pltpu.SemaphoreType.DMA((chunks,)),
        ],
        compiler_params=pltpu.CompilerParams(
            collective_id=0, has_side_effects=True, vmem_limit_bytes=60 << 20
        ),
        name="sections",
    )(pattern[0], bias, inputs.reshape(micro * batch, columns), weights[0])
    return out.reshape(1, micro, batch, columns)


def solution(mesh):
    return jax.shard_map(
        functools.partial(per_device, mesh.shape["pipe"], mesh.shape["neuron"]),
        mesh=mesh,
        in_specs=(
            P(None, None, "neuron"),
            P("pipe", "neuron", None, None, None),
            P("pipe", "neuron", None),
            P("pipe", "neuron"),
        ),
        out_specs=P("pipe", None, None, "neuron"),
        check_vma=False,
    )
```

```python
import functools

import jax
import jax.numpy as jnp
from jax import lax
from jax.experimental import pallas as pl
from jax.experimental.pallas import tpu as pltpu
from jax.sharding import PartitionSpec as P

MESH = pl.DeviceIdType.MESH
UNIT = 16
OFFLOAD = 16
DIRECT_EDGE = 0
FIRST_AHEAD = 5
EVEN_AHEAD = 4
PASS_AT = 0


def kernel(
    sections, groups, units, rows, blocks, entries, width,
    pattern_hbm, bias_hbm, x_ref, w_ref, result,
    pattern_ref, bias_ref, ids, landing, work, held,
    small_sem, w_sem, in_sem, own_sem, side_sem, pass_sem, send_sem,
):
    section = lax.axis_index("pipe")
    group = lax.axis_index("neuron")
    right = lax.rem(group + 1, groups)
    left = lax.rem(group + groups - 1, groups)
    even = lax.rem(section, 2) == 0
    first = section == 0
    last = section == sections - 1
    later_even = jnp.logical_and(even, section > 0)
    odd = jnp.logical_not(even)
    odd_sends = jnp.logical_and(odd, section < sections - 1)
    beside = (group, left, right)

    barrier = pltpu.get_barrier_semaphore()

    def signal(to_section, to_group):
        pl.semaphore_signal(
            barrier, inc=1, device_id={"pipe": to_section, "neuron": to_group}, device_id_type=MESH
        )

    @pl.when(even)
    def _():
        signal(section, left)
        signal(section, right)
        for to in beside:
            signal(section + 1, to)

    @pl.when(first)
    def _():
        signal(sections - 1, left)
        signal(sections - 1, right)

    @pl.when(last)
    def _():
        signal(0, left)
        signal(0, right)

    @pl.when(later_even)
    def _():
        for to in beside:
            signal(section - 1, to)

    @pl.when(odd)
    def _():
        for to in beside:
            signal(section - 1, to)

    @pl.when(odd_sends)
    def _():
        for to in beside:
            signal(section + 1, to)

    pattern_copy = pltpu.make_async_copy(pattern_hbm, pattern_ref, small_sem.at[0])
    bias_copy = pltpu.make_async_copy(bias_hbm, bias_ref, small_sem.at[1])
    pattern_copy.start()
    bias_copy.start()

    def unit_rows(u):
        return pl.ds(pl.multiple_of(u * rows, rows), rows)

    def load_copy(u):
        return pltpu.make_async_copy(x_ref.at[unit_rows(u)], landing.at[1, unit_rows(u)], in_sem.at[u])

    def weight_copy(j):
        return pltpu.make_async_copy(w_ref.at[j], held.at[j], w_sem.at[j])

    @pl.when(first)
    def _():
        for u in range(units):
            load_copy(u).start()

    for j in range(blocks):
        weight_copy(j).start()

    @pl.when(first)
    def _():
        pl.semaphore_wait(barrier, 7)

    @pl.when(later_even)
    def _():
        pl.semaphore_wait(barrier, 8)

    @pl.when(odd_sends)
    def _():
        pl.semaphore_wait(barrier, 6)

    @pl.when(last)
    def _():
        pl.semaphore_wait(barrier, 5)

    def remote(src, dst, send, recv, to_section, to_group):
        return pltpu.make_async_remote_copy(
            src_ref=src, dst_ref=dst, send_sem=send, recv_sem=recv,
            device_id={"pipe": to_section, "neuron": to_group}, device_id_type=MESH,
        )

    def pass_copy(u, side):
        return remote(
            landing.at[1, unit_rows(u)], landing.at[2 * side, unit_rows(u)],
            pass_sem.at[u, side], side_sem.at[u, side], section, (right, left)[side],
        )

    def input_copy(u, side):
        return remote(
            x_ref.at[unit_rows(u)], landing.at[2 * side, unit_rows(u)],
            pass_sem.at[u, side], side_sem.at[u, side], 0, (right, left)[side],
        )

    def down_copy(u):
        return remote(
            result.at[unit_rows(u)], landing.at[1, unit_rows(u)],
            send_sem.at[u, 2], own_sem.at[u], section + 1, group,
        )

    def down_side_copy(u, side):
        return remote(
            result.at[unit_rows(u)], landing.at[2 * side, unit_rows(u)],
            send_sem.at[u, side], side_sem.at[u, side], section + 1, (right, left)[side],
        )

    def direct(side):
        if not DIRECT_EDGE:
            return section < 0
        return lax.rem((group, left)[side], DIRECT_EDGE) == DIRECT_EDGE - 1

    passes = [jnp.logical_and(later_even, jnp.logical_not(direct(side))) for side in range(2)]
    sends_side = [jnp.logical_or(even, jnp.logical_and(odd_sends, direct(side))) for side in range(2)]

    def pass_first(u):
        for side in range(2):
            pass_copy(u, side).start()

    def pass_even(u):
        down_copy(u).wait_recv()
        for side in range(2):
            @pl.when(passes[side])
            def _():
                pass_copy(u, side).start()

    def pass_on(u):
        if OFFLOAD > FIRST_AHEAD:
            @pl.when(jnp.logical_and(first, u + FIRST_AHEAD < OFFLOAD))
            def _():
                pass_first(u + FIRST_AHEAD)

        @pl.when(jnp.logical_and(later_even, u + EVEN_AHEAD < units))
        def _():
            pass_even(u + EVEN_AHEAD)

    @pl.when(first)
    def _():
        for u in range(min(FIRST_AHEAD, OFFLOAD)):
            load_copy(u).wait()
            pass_first(u)
        for u in range(min(FIRST_AHEAD, OFFLOAD), units):
            load_copy(u).wait()

    @pl.when(last)
    def _():
        for u in range(OFFLOAD, units):
            for side in range(2):
                input_copy(u, side).start()

    pattern_copy.wait()
    base = (group - 1) * blocks
    total = groups * blocks

    @pl.loop(0, blocks)
    def _(j):
        for k in range(entries):
            near = lax.rem(pattern_ref[j, k] - base + total, total)
            ids[j, k] = jnp.minimum(near, 3 * blocks - 1)

    @pl.when(later_even)
    def _():
        for u in range(EVEN_AHEAD):
            pass_even(u)

    @pl.loop(0, units)
    def _(u):
        if not PASS_AT:
            pass_on(u)

        @pl.when(odd)
        def _():
            down_copy(u).wait_recv()

        for side in range(2):
            pass_copy(u, side).wait_recv()

        @pl.when(u == 0)
        def _():
            bias_copy.wait()
            for j in range(blocks):
                weight_copy(j).wait()

        for side in range(3):
            for b in range(blocks):
                work[side * blocks + b] = landing[side, unit_rows(u), b * width : (b + 1) * width]

        for j in range(blocks):
            if PASS_AT and j == PASS_AT:
                pass_on(u)
            picked = jnp.concatenate([work[ids[j, k]] for k in range(entries)], axis=1)
            summed = jnp.dot(
                picked, held[j].reshape(entries * width, width), preferred_element_type=jnp.float32
            )
            summed = summed + bias_ref[:, j * width : (j + 1) * width]
            result[unit_rows(u), j * width : (j + 1) * width] = jnp.maximum(summed, 0.0).astype(jnp.bfloat16)

        for side in range(2):
            @pl.when(sends_side[side])
            def _():
                down_side_copy(u, side).start()

        @pl.when(jnp.logical_not(last))
        def _():
            down_copy(u).start()

    def drain_side(u, side):
        @pl.when(jnp.logical_or(jnp.logical_and(first, u < OFFLOAD), passes[side]))
        def _():
            pass_copy(u, side).wait_send()

        @pl.when(sends_side[side])
        def _():
            down_side_copy(u, side).wait_send()

    @pl.when(jnp.logical_not(last))
    def _():
        @pl.loop(0, units)
        def _(u):
            drain_side(u, 0)
            drain_side(u, 1)
            down_copy(u).wait_send()

    if OFFLOAD < units:
        @pl.when(last)
        def _():
            @pl.loop(OFFLOAD, units)
            def _(u):
                input_copy(u, 0).wait_send()
                input_copy(u, 1).wait_send()


def per_device(sections, groups, inputs, weights, pattern, bias):
    micro, batch, columns = inputs.shape
    blocks, entries, width = weights.shape[1:4]
    units = micro * batch // UNIT
    dma = pltpu.SemaphoreType.DMA
    out = pl.pallas_call(
        functools.partial(
            kernel, sections, groups, units, UNIT, blocks, entries, width
        ),
        out_shape=pltpu.VMEM((micro * batch, columns), jnp.bfloat16),
        in_specs=[pl.BlockSpec(memory_space=pl.ANY)] * 4,
        out_specs=pl.BlockSpec(memory_space=pltpu.VMEM),
        scratch_shapes=[
            pltpu.SMEM((blocks, entries), jnp.int32),
            pltpu.VMEM((1, columns), jnp.float32),
            pltpu.SMEM((blocks, entries), jnp.int32),
            pltpu.VMEM((3, micro * batch, columns), jnp.bfloat16),
            pltpu.VMEM((3 * blocks, UNIT, width), jnp.bfloat16),
            pltpu.VMEM((blocks, entries, width, width), jnp.bfloat16),
            dma((2,)),
            dma((blocks,)),
            dma((units,)),
            dma((units,)),
            dma((units, 2)),
            dma((units, 2)),
            dma((units, 3)),
        ],
        compiler_params=pltpu.CompilerParams(
            collective_id=0, has_side_effects=True, vmem_limit_bytes=60 << 20
        ),
        name="sections",
    )(pattern[0], bias, inputs.reshape(micro * batch, columns), weights[0])
    return out.reshape(1, micro, batch, columns)


def solution(mesh):
    return jax.shard_map(
        functools.partial(per_device, mesh.shape["pipe"], mesh.shape["neuron"]),
        mesh=mesh,
        in_specs=(
            P(None, None, "neuron"),
            P("pipe", "neuron", None, None, None),
            P("pipe", "neuron", None),
            P("pipe", "neuron"),
        ),
        out_specs=P("pipe", None, None, "neuron"),
        check_vma=False,
    )
```

```python
import functools

import jax
import jax.numpy as jnp
from jax import lax
from jax.experimental import pallas as pl
from jax.experimental.pallas import tpu as pltpu
from jax.sharding import PartitionSpec as P

MESH = pl.DeviceIdType.MESH
UNIT = 16
DIRECT_EDGE = 32
OFFLOAD = 2
FIRST_AHEAD = 5
EVEN_AHEAD = 4
NEAR_AHEAD = 2


def kernel(
    sections, groups, units, rows, blocks, entries, width,
    pattern_hbm, bias_hbm, x_ref, w_ref, result,
    pattern_ref, bias_ref, ids, landing, work, held,
    small_sem, w_sem, in_sem, own_sem, side_sem, pass_sem, send_sem,
):
    section = lax.axis_index("pipe")
    group = lax.axis_index("neuron")
    right = lax.rem(group + 1, groups)
    left = lax.rem(group + groups - 1, groups)
    even = lax.rem(section, 2) == 0
    first = section == 0
    last = section == sections - 1
    later_even = jnp.logical_and(even, section > 0)
    odd = jnp.logical_not(even)
    odd_sends = jnp.logical_and(odd, section < sections - 1)
    beside = (group, left, right)

    barrier = pltpu.get_barrier_semaphore()

    def signal(to_section, to_group):
        pl.semaphore_signal(
            barrier, inc=1, device_id={"pipe": to_section, "neuron": to_group}, device_id_type=MESH
        )

    @pl.when(even)
    def _():
        signal(section, left)
        signal(section, right)
        for to in beside:
            signal(section + 1, to)

    @pl.when(first)
    def _():
        signal(sections - 1, left)
        signal(sections - 1, right)

    @pl.when(last)
    def _():
        signal(0, left)
        signal(0, right)

    @pl.when(later_even)
    def _():
        for to in beside:
            signal(section - 1, to)

    @pl.when(odd)
    def _():
        for to in beside:
            signal(section - 1, to)

    @pl.when(odd_sends)
    def _():
        for to in beside:
            signal(section + 1, to)

    pattern_copy = pltpu.make_async_copy(pattern_hbm, pattern_ref, small_sem.at[0])
    bias_copy = pltpu.make_async_copy(bias_hbm, bias_ref, small_sem.at[1])
    pattern_copy.start()
    bias_copy.start()

    def unit_rows(u):
        return pl.ds(pl.multiple_of(u * rows, rows), rows)

    def load_copy(u):
        return pltpu.make_async_copy(x_ref.at[unit_rows(u)], landing.at[1, unit_rows(u)], in_sem.at[u])

    def weight_copy(j):
        return pltpu.make_async_copy(w_ref.at[j], held.at[j], w_sem.at[j])

    @pl.when(first)
    def _():
        for u in range(units):
            load_copy(u).start()

    for j in range(blocks):
        weight_copy(j).start()

    @pl.when(first)
    def _():
        pl.semaphore_wait(barrier, 7)

    @pl.when(later_even)
    def _():
        pl.semaphore_wait(barrier, 8)

    @pl.when(odd_sends)
    def _():
        pl.semaphore_wait(barrier, 6)

    @pl.when(last)
    def _():
        pl.semaphore_wait(barrier, 5)

    def remote(src, dst, send, recv, to_section, to_group):
        return pltpu.make_async_remote_copy(
            src_ref=src, dst_ref=dst, send_sem=send, recv_sem=recv,
            device_id={"pipe": to_section, "neuron": to_group}, device_id_type=MESH,
        )

    def pass_copy(u, side):
        return remote(
            landing.at[1, unit_rows(u)], landing.at[2 * side, unit_rows(u)],
            pass_sem.at[u, side], side_sem.at[u, side], section, (right, left)[side],
        )

    def input_copy(u, side):
        return remote(
            x_ref.at[unit_rows(u)], landing.at[2 * side, unit_rows(u)],
            pass_sem.at[u, side], side_sem.at[u, side], 0, (right, left)[side],
        )

    def down_copy(u):
        return remote(
            result.at[unit_rows(u)], landing.at[1, unit_rows(u)],
            send_sem.at[u, 2], own_sem.at[u], section + 1, group,
        )

    def down_side_copy(u, side):
        return remote(
            result.at[unit_rows(u)], landing.at[2 * side, unit_rows(u)],
            send_sem.at[u, side], side_sem.at[u, side], section + 1, (right, left)[side],
        )

    direct = [lax.rem(border, DIRECT_EDGE) == DIRECT_EDGE - 1 for border in (group, left)]
    near = jnp.logical_or(direct[0], direct[1])
    passes = [jnp.logical_and(later_even, jnp.logical_not(direct[side])) for side in range(2)]
    sends_side = [jnp.logical_or(even, jnp.logical_and(odd_sends, direct[side])) for side in range(2)]

    def by_first(u, side):
        return jnp.logical_or(u < OFFLOAD, jnp.logical_not(direct[side]))

    def pass_first(u):
        for side in range(2):
            @pl.when(by_first(u, side))
            def _():
                pass_copy(u, side).start()

    def pass_even(u):
        down_copy(u).wait_recv()
        for side in range(2):
            @pl.when(passes[side])
            def _():
                pass_copy(u, side).start()

    def pass_on(u):
        @pl.when(jnp.logical_and(first, u + FIRST_AHEAD < units))
        def _():
            pass_first(u + FIRST_AHEAD)

        for some, ahead in ((near, NEAR_AHEAD), (jnp.logical_not(near), EVEN_AHEAD)):
            @pl.when(jnp.logical_and(jnp.logical_and(later_even, some), u + ahead < units))
            def _():
                pass_even(u + ahead)

    @pl.when(first)
    def _():
        for u in range(FIRST_AHEAD):
            load_copy(u).wait()
            pass_first(u)
        for u in range(FIRST_AHEAD, units):
            load_copy(u).wait()

    @pl.when(last)
    def _():
        for side in range(2):
            @pl.when(direct[side])
            def _():
                for u in range(OFFLOAD, units):
                    input_copy(u, side).start()

    pattern_copy.wait()
    base = (group - 1) * blocks
    total = groups * blocks

    @pl.loop(0, blocks)
    def _(j):
        for k in range(entries):
            near = lax.rem(pattern_ref[j, k] - base + total, total)
            ids[j, k] = jnp.minimum(near, 3 * blocks - 1)

    @pl.when(later_even)
    def _():
        for u in range(NEAR_AHEAD):
            pass_even(u)

        @pl.when(jnp.logical_not(near))
        def _():
            for u in range(NEAR_AHEAD, EVEN_AHEAD):
                pass_even(u)

    @pl.loop(0, units)
    def _(u):
        pass_on(u)

        @pl.when(odd)
        def _():
            down_copy(u).wait_recv()

        for side in range(2):
            pass_copy(u, side).wait_recv()

        @pl.when(u == 0)
        def _():
            bias_copy.wait()
            for j in range(blocks):
                weight_copy(j).wait()

        for side in range(3):
            for b in range(blocks):
                work[side * blocks + b] = landing[side, unit_rows(u), b * width : (b + 1) * width]

        for j in range(blocks):
            picked = jnp.concatenate([work[ids[j, k]] for k in range(entries)], axis=1)
            summed = jnp.dot(
                picked, held[j].reshape(entries * width, width), preferred_element_type=jnp.float32
            )
            summed = summed + bias_ref[:, j * width : (j + 1) * width]
            result[unit_rows(u), j * width : (j + 1) * width] = jnp.maximum(summed, 0.0).astype(jnp.bfloat16)

        @pl.when(odd_sends)
        def _():
            down_copy(u).start()

        for side in range(2):
            @pl.when(sends_side[side])
            def _():
                down_side_copy(u, side).start()

        @pl.when(even)
        def _():
            down_copy(u).start()

    def drain_side(u, side):
        @pl.when(jnp.logical_or(jnp.logical_and(first, by_first(u, side)), passes[side]))
        def _():
            pass_copy(u, side).wait_send()

        @pl.when(sends_side[side])
        def _():
            down_side_copy(u, side).wait_send()

    @pl.when(jnp.logical_not(last))
    def _():
        @pl.loop(0, units)
        def _(u):
            drain_side(u, 0)
            drain_side(u, 1)
            down_copy(u).wait_send()

    @pl.when(last)
    def _():
        for side in range(2):
            @pl.when(direct[side])
            def _():
                @pl.loop(OFFLOAD, units)
                def _(u):
                    input_copy(u, side).wait_send()


def per_device(sections, groups, inputs, weights, pattern, bias):
    micro, batch, columns = inputs.shape
    blocks, entries, width = weights.shape[1:4]
    units = micro * batch // UNIT
    dma = pltpu.SemaphoreType.DMA
    out = pl.pallas_call(
        functools.partial(
            kernel, sections, groups, units, UNIT, blocks, entries, width
        ),
        out_shape=pltpu.VMEM((micro * batch, columns), jnp.bfloat16),
        in_specs=[pl.BlockSpec(memory_space=pl.ANY)] * 4,
        out_specs=pl.BlockSpec(memory_space=pltpu.VMEM),
        scratch_shapes=[
            pltpu.SMEM((blocks, entries), jnp.int32),
            pltpu.VMEM((1, columns), jnp.float32),
            pltpu.SMEM((blocks, entries), jnp.int32),
            pltpu.VMEM((3, micro * batch, columns), jnp.bfloat16),
            pltpu.VMEM((3 * blocks, UNIT, width), jnp.bfloat16),
            pltpu.VMEM((blocks, entries, width, width), jnp.bfloat16),
            dma((2,)),
            dma((blocks,)),
            dma((units,)),
            dma((units,)),
            dma((units, 2)),
            dma((units, 2)),
            dma((units, 3)),
        ],
        compiler_params=pltpu.CompilerParams(
            collective_id=0, has_side_effects=True, vmem_limit_bytes=60 << 20
        ),
        name="sections",
    )(pattern[0], bias, inputs.reshape(micro * batch, columns), weights[0])
    return out.reshape(1, micro, batch, columns)


def solution(mesh):
    return jax.shard_map(
        functools.partial(per_device, mesh.shape["pipe"], mesh.shape["neuron"]),
        mesh=mesh,
        in_specs=(
            P(None, None, "neuron"),
            P("pipe", "neuron", None, None, None),
            P("pipe", "neuron", None),
            P("pipe", "neuron"),
        ),
        out_specs=P("pipe", None, None, "neuron"),
        check_vma=False,
    )
```

```python
import functools

import jax
import jax.numpy as jnp
from jax import lax
from jax.experimental import pallas as pl
from jax.experimental.pallas import tpu as pltpu
from jax.sharding import PartitionSpec as P

MESH = pl.DeviceIdType.MESH
UNIT = 16
DIRECT_EDGE = 32
OFFLOAD = 2
FIRST_AHEAD = 5
EVEN_AHEAD = 4
NEAR_AHEAD = 2


def kernel(
    sections, groups, units, rows, blocks, entries, width,
    pattern_hbm, bias_hbm, x_ref, w_ref, result,
    pattern_ref, bias_ref, ids, landing, work, held,
    small_sem, w_sem, in_sem, own_sem, side_sem, pass_sem, send_sem,
):
    section = lax.axis_index("pipe")
    group = lax.axis_index("neuron")
    right = lax.rem(group + 1, groups)
    left = lax.rem(group + groups - 1, groups)
    even = lax.rem(section, 2) == 0
    first = section == 0
    last = section == sections - 1
    later_even = jnp.logical_and(even, section > 0)
    odd = jnp.logical_not(even)
    odd_sends = jnp.logical_and(odd, section < sections - 1)
    beside = (group, left, right)

    direct = [lax.rem(border, DIRECT_EDGE) == DIRECT_EDGE - 1 for border in (group, left)]
    near = jnp.logical_or(direct[0], direct[1])

    barrier = pltpu.get_barrier_semaphore()

    def signal(to_section, to_group):
        pl.semaphore_signal(
            barrier, inc=1, device_id={"pipe": to_section, "neuron": to_group}, device_id_type=MESH
        )

    @pl.when(even)
    def _():
        signal(section, left)
        signal(section, right)
        for to in beside:
            signal(section + 1, to)

    @pl.when(later_even)
    def _():
        signal(section - 1, group)

    @pl.when(odd)
    def _():
        for to in beside:
            signal(section - 1, to)

    @pl.when(odd_sends)
    def _():
        signal(section + 1, group)

    for side in range(2):
        to = (right, left)[side]
        for some, to_section in (
            (first, sections - 1), (last, 0), (later_even, section - 1), (odd_sends, section + 1)
        ):
            @pl.when(jnp.logical_and(some, direct[side]))
            def _():
                signal(to_section, to)

    pattern_copy = pltpu.make_async_copy(pattern_hbm, pattern_ref, small_sem.at[0])
    bias_copy = pltpu.make_async_copy(bias_hbm, bias_ref, small_sem.at[1])
    pattern_copy.start()
    bias_copy.start()

    def unit_rows(u):
        return pl.ds(pl.multiple_of(u * rows, rows), rows)

    def load_copy(u):
        return pltpu.make_async_copy(x_ref.at[unit_rows(u)], landing.at[1, unit_rows(u)], in_sem.at[u])

    def weight_copy(j):
        return pltpu.make_async_copy(w_ref.at[j], held.at[j], w_sem.at[j])

    @pl.when(first)
    def _():
        for u in range(units):
            load_copy(u).start()

    for j in range(blocks):
        weight_copy(j).start()

    for some, count in ((first, 5), (later_even, 6), (odd_sends, 4), (last, 3)):
        @pl.when(jnp.logical_and(some, near))
        def _():
            pl.semaphore_wait(barrier, count + 1)

        @pl.when(jnp.logical_and(some, jnp.logical_not(near)))
        def _():
            pl.semaphore_wait(barrier, count)

    def remote(src, dst, send, recv, to_section, to_group):
        return pltpu.make_async_remote_copy(
            src_ref=src, dst_ref=dst, send_sem=send, recv_sem=recv,
            device_id={"pipe": to_section, "neuron": to_group}, device_id_type=MESH,
        )

    def pass_copy(u, side):
        return remote(
            landing.at[1, unit_rows(u)], landing.at[2 * side, unit_rows(u)],
            pass_sem.at[u, side], side_sem.at[u, side], section, (right, left)[side],
        )

    def input_copy(u, side):
        return remote(
            x_ref.at[unit_rows(u)], landing.at[2 * side, unit_rows(u)],
            pass_sem.at[u, side], side_sem.at[u, side], 0, (right, left)[side],
        )

    def down_copy(u):
        return remote(
            result.at[unit_rows(u)], landing.at[1, unit_rows(u)],
            send_sem.at[u, 2], own_sem.at[u], section + 1, group,
        )

    def down_side_copy(u, side):
        return remote(
            result.at[unit_rows(u)], landing.at[2 * side, unit_rows(u)],
            send_sem.at[u, side], side_sem.at[u, side], section + 1, (right, left)[side],
        )

    passes = [jnp.logical_and(later_even, jnp.logical_not(direct[side])) for side in range(2)]
    sends_side = [jnp.logical_or(even, jnp.logical_and(odd_sends, direct[side])) for side in range(2)]

    def by_first(u, side):
        return jnp.logical_or(u < OFFLOAD, jnp.logical_not(direct[side]))

    def pass_first(u):
        for side in range(2):
            @pl.when(by_first(u, side))
            def _():
                pass_copy(u, side).start()

    def pass_even(u):
        down_copy(u).wait_recv()
        for side in range(2):
            @pl.when(passes[side])
            def _():
                pass_copy(u, side).start()

    def pass_on(u):
        @pl.when(jnp.logical_and(first, u + FIRST_AHEAD < units))
        def _():
            pass_first(u + FIRST_AHEAD)

        for some, ahead in ((near, NEAR_AHEAD), (jnp.logical_not(near), EVEN_AHEAD)):
            @pl.when(jnp.logical_and(jnp.logical_and(later_even, some), u + ahead < units))
            def _():
                pass_even(u + ahead)

    @pl.when(first)
    def _():
        for u in range(FIRST_AHEAD):
            load_copy(u).wait()
            pass_first(u)
        for u in range(FIRST_AHEAD, units):
            load_copy(u).wait()

    @pl.when(last)
    def _():
        for side in range(2):
            @pl.when(direct[side])
            def _():
                for u in range(OFFLOAD, units):
                    input_copy(u, side).start()

    pattern_copy.wait()
    base = (group - 1) * blocks
    total = groups * blocks

    @pl.loop(0, blocks)
    def _(j):
        for k in range(entries):
            near = lax.rem(pattern_ref[j, k] - base + total, total)
            ids[j, k] = jnp.minimum(near, 3 * blocks - 1)

    @pl.when(later_even)
    def _():
        for u in range(NEAR_AHEAD):
            pass_even(u)

        @pl.when(jnp.logical_not(near))
        def _():
            for u in range(NEAR_AHEAD, EVEN_AHEAD):
                pass_even(u)

    @pl.loop(0, units)
    def _(u):
        pass_on(u)

        @pl.when(odd)
        def _():
            down_copy(u).wait_recv()

        for side in range(2):
            pass_copy(u, side).wait_recv()

        @pl.when(u == 0)
        def _():
            bias_copy.wait()
            for j in range(blocks):
                weight_copy(j).wait()

        for side in range(3):
            for b in range(blocks):
                work[side * blocks + b] = landing[side, unit_rows(u), b * width : (b + 1) * width]

        for j in range(blocks):
            picked = jnp.concatenate([work[ids[j, k]] for k in range(entries)], axis=1)
            summed = jnp.dot(
                picked, held[j].reshape(entries * width, width), preferred_element_type=jnp.float32
            )
            summed = summed + bias_ref[:, j * width : (j + 1) * width]
            result[unit_rows(u), j * width : (j + 1) * width] = jnp.maximum(summed, 0.0).astype(jnp.bfloat16)

        @pl.when(odd_sends)
        def _():
            down_copy(u).start()

        for side in range(2):
            @pl.when(sends_side[side])
            def _():
                down_side_copy(u, side).start()

        @pl.when(even)
        def _():
            down_copy(u).start()

    def drain_side(u, side):
        @pl.when(jnp.logical_or(jnp.logical_and(first, by_first(u, side)), passes[side]))
        def _():
            pass_copy(u, side).wait_send()

        @pl.when(sends_side[side])
        def _():
            down_side_copy(u, side).wait_send()

    @pl.when(jnp.logical_not(last))
    def _():
        @pl.loop(0, units)
        def _(u):
            drain_side(u, 0)
            drain_side(u, 1)
            down_copy(u).wait_send()

    @pl.when(last)
    def _():
        for side in range(2):
            @pl.when(direct[side])
            def _():
                @pl.loop(OFFLOAD, units)
                def _(u):
                    input_copy(u, side).wait_send()


def per_device(sections, groups, inputs, weights, pattern, bias):
    micro, batch, columns = inputs.shape
    blocks, entries, width = weights.shape[1:4]
    units = micro * batch // UNIT
    dma = pltpu.SemaphoreType.DMA
    out = pl.pallas_call(
        functools.partial(
            kernel, sections, groups, units, UNIT, blocks, entries, width
        ),
        out_shape=pltpu.VMEM((micro * batch, columns), jnp.bfloat16),
        in_specs=[pl.BlockSpec(memory_space=pl.ANY)] * 4,
        out_specs=pl.BlockSpec(memory_space=pltpu.VMEM),
        scratch_shapes=[
            pltpu.SMEM((blocks, entries), jnp.int32),
            pltpu.VMEM((1, columns), jnp.float32),
            pltpu.SMEM((blocks, entries), jnp.int32),
            pltpu.VMEM((3, micro * batch, columns), jnp.bfloat16),
            pltpu.VMEM((3 * blocks, UNIT, width), jnp.bfloat16),
            pltpu.VMEM((blocks, entries, width, width), jnp.bfloat16),
            dma((2,)),
            dma((blocks,)),
            dma((units,)),
            dma((units,)),
            dma((units, 2)),
            dma((units, 2)),
            dma((units, 3)),
        ],
        compiler_params=pltpu.CompilerParams(
            collective_id=0, has_side_effects=True, vmem_limit_bytes=60 << 20
        ),
        name="sections",
    )(pattern[0], bias, inputs.reshape(micro * batch, columns), weights[0])
    return out.reshape(1, micro, batch, columns)


def solution(mesh):
    return jax.shard_map(
        functools.partial(per_device, mesh.shape["pipe"], mesh.shape["neuron"]),
        mesh=mesh,
        in_specs=(
            P(None, None, "neuron"),
            P("pipe", "neuron", None, None, None),
            P("pipe", "neuron", None),
            P("pipe", "neuron"),
        ),
        out_specs=P("pipe", None, None, "neuron"),
        check_vma=False,
    )
```

```python
import functools

import jax
import jax.numpy as jnp
from jax import lax
from jax.experimental import pallas as pl
from jax.experimental.pallas import tpu as pltpu
from jax.sharding import PartitionSpec as P

MESH = pl.DeviceIdType.MESH
UNIT = 16
DIRECT_EDGE = 32
OFFLOAD = 2
FIRST_AHEAD = 4
EVEN_AHEAD = 4
NEAR_AHEAD = 2


def kernel(
    sections, groups, units, rows, blocks, entries, width,
    pattern_hbm, bias_hbm, x_ref, w_ref, result,
    pattern_ref, bias_ref, ids, landing, work, held,
    small_sem, w_sem, in_sem, own_sem, side_sem, pass_sem, send_sem,
):
    section = lax.axis_index("pipe")
    group = lax.axis_index("neuron")
    right = lax.rem(group + 1, groups)
    left = lax.rem(group + groups - 1, groups)
    even = lax.rem(section, 2) == 0
    first = section == 0
    last = section == sections - 1
    later_even = jnp.logical_and(even, section > 0)
    odd = jnp.logical_not(even)
    odd_sends = jnp.logical_and(odd, section < sections - 1)
    beside = (group, left, right)

    direct = [lax.rem(border, DIRECT_EDGE) == DIRECT_EDGE - 1 for border in (group, left)]
    near = jnp.logical_or(direct[0], direct[1])

    barrier = pltpu.get_barrier_semaphore()

    def signal(to_section, to_group):
        pl.semaphore_signal(
            barrier, inc=1, device_id={"pipe": to_section, "neuron": to_group}, device_id_type=MESH
        )

    @pl.when(even)
    def _():
        signal(section, left)
        signal(section, right)
        for to in beside:
            signal(section + 1, to)

    @pl.when(later_even)
    def _():
        signal(section - 1, group)

    @pl.when(odd)
    def _():
        for to in beside:
            signal(section - 1, to)

    @pl.when(odd_sends)
    def _():
        signal(section + 1, group)

    for side in range(2):
        to = (right, left)[side]
        for some, to_section in (
            (first, sections - 1), (last, 0), (later_even, section - 1), (odd_sends, section + 1)
        ):
            @pl.when(jnp.logical_and(some, direct[side]))
            def _():
                signal(to_section, to)

    pattern_copy = pltpu.make_async_copy(pattern_hbm, pattern_ref, small_sem.at[0])
    bias_copy = pltpu.make_async_copy(bias_hbm, bias_ref, small_sem.at[1])
    pattern_copy.start()
    bias_copy.start()

    def unit_rows(u):
        return pl.ds(pl.multiple_of(u * rows, rows), rows)

    def load_copy(u):
        return pltpu.make_async_copy(x_ref.at[unit_rows(u)], landing.at[1, unit_rows(u)], in_sem.at[u])

    def weight_copy(j):
        return pltpu.make_async_copy(w_ref.at[j], held.at[j], w_sem.at[j])

    @pl.when(first)
    def _():
        for u in range(units):
            load_copy(u).start()

    for j in range(blocks):
        weight_copy(j).start()

    for some, count in ((first, 5), (later_even, 6), (odd_sends, 4), (last, 3)):
        @pl.when(jnp.logical_and(some, near))
        def _():
            pl.semaphore_wait(barrier, count + 1)

        @pl.when(jnp.logical_and(some, jnp.logical_not(near)))
        def _():
            pl.semaphore_wait(barrier, count)

    def remote(src, dst, send, recv, to_section, to_group):
        return pltpu.make_async_remote_copy(
            src_ref=src, dst_ref=dst, send_sem=send, recv_sem=recv,
            device_id={"pipe": to_section, "neuron": to_group}, device_id_type=MESH,
        )

    def pass_copy(u, side):
        return remote(
            landing.at[1, unit_rows(u)], landing.at[2 * side, unit_rows(u)],
            pass_sem.at[u, side], side_sem.at[u, side], section, (right, left)[side],
        )

    def input_copy(u, side):
        return remote(
            x_ref.at[unit_rows(u)], landing.at[2 * side, unit_rows(u)],
            pass_sem.at[u, side], side_sem.at[u, side], 0, (right, left)[side],
        )

    def down_copy(u):
        return remote(
            result.at[unit_rows(u)], landing.at[1, unit_rows(u)],
            send_sem.at[u, 2], own_sem.at[u], section + 1, group,
        )

    def down_side_copy(u, side):
        return remote(
            result.at[unit_rows(u)], landing.at[2 * side, unit_rows(u)],
            send_sem.at[u, side], side_sem.at[u, side], section + 1, (right, left)[side],
        )

    passes = [jnp.logical_and(later_even, jnp.logical_not(direct[side])) for side in range(2)]
    sends_side = [jnp.logical_or(even, jnp.logical_and(odd_sends, direct[side])) for side in range(2)]

    def by_first(u, side):
        return jnp.logical_or(u < OFFLOAD, jnp.logical_not(direct[side]))

    def pass_first(u):
        for side in range(2):
            @pl.when(by_first(u, side))
            def _():
                pass_copy(u, side).start()

    def pass_even(u):
        down_copy(u).wait_recv()
        for side in range(2):
            @pl.when(passes[side])
            def _():
                pass_copy(u, side).start()

    def pass_on(u):
        @pl.when(jnp.logical_and(first, u + FIRST_AHEAD < units))
        def _():
            pass_first(u + FIRST_AHEAD)

        for some, ahead in ((near, NEAR_AHEAD), (jnp.logical_not(near), EVEN_AHEAD)):
            @pl.when(jnp.logical_and(jnp.logical_and(later_even, some), u + ahead < units))
            def _():
                pass_even(u + ahead)

    @pl.when(first)
    def _():
        for u in range(FIRST_AHEAD):
            load_copy(u).wait()
            pass_first(u)
        for u in range(FIRST_AHEAD, units):
            load_copy(u).wait()

    @pl.when(last)
    def _():
        for side in range(2):
            @pl.when(direct[side])
            def _():
                for u in range(OFFLOAD, units):
                    input_copy(u, side).start()

                @pl.loop(OFFLOAD, units)
                def _(u):
                    input_copy(u, side).wait_send()

    pattern_copy.wait()
    base = (group - 1) * blocks
    total = groups * blocks

    @pl.loop(0, blocks)
    def _(j):
        for k in range(entries):
            near = lax.rem(pattern_ref[j, k] - base + total, total)
            ids[j, k] = jnp.minimum(near, 3 * blocks - 1)

    @pl.when(later_even)
    def _():
        for u in range(NEAR_AHEAD):
            pass_even(u)

        @pl.when(jnp.logical_not(near))
        def _():
            for u in range(NEAR_AHEAD, EVEN_AHEAD):
                pass_even(u)

    @pl.loop(0, units)
    def _(u):
        pass_on(u)

        @pl.when(odd)
        def _():
            down_copy(u).wait_recv()

        for side in range(2):
            pass_copy(u, side).wait_recv()

        @pl.when(u == 0)
        def _():
            bias_copy.wait()
            for j in range(blocks):
                weight_copy(j).wait()

        for side in range(3):
            for b in range(blocks):
                work[side * blocks + b] = landing[side, unit_rows(u), b * width : (b + 1) * width]

        for j in range(blocks):
            picked = jnp.concatenate([work[ids[j, k]] for k in range(entries)], axis=1)
            summed = jnp.dot(
                picked, held[j].reshape(entries * width, width), preferred_element_type=jnp.float32
            )
            summed = summed + bias_ref[:, j * width : (j + 1) * width]
            result[unit_rows(u), j * width : (j + 1) * width] = jnp.maximum(summed, 0.0).astype(jnp.bfloat16)

        @pl.when(odd_sends)
        def _():
            down_copy(u).start()

        for side in range(2):
            @pl.when(sends_side[side])
            def _():
                down_side_copy(u, side).start()

        @pl.when(even)
        def _():
            down_copy(u).start()

    def drain_side(u, side):
        @pl.when(jnp.logical_or(jnp.logical_and(first, by_first(u, side)), passes[side]))
        def _():
            pass_copy(u, side).wait_send()

        @pl.when(sends_side[side])
        def _():
            down_side_copy(u, side).wait_send()

    @pl.when(jnp.logical_not(last))
    def _():
        @pl.loop(0, units)
        def _(u):
            drain_side(u, 0)
            drain_side(u, 1)
            down_copy(u).wait_send()


def per_device(sections, groups, inputs, weights, pattern, bias):
    micro, batch, columns = inputs.shape
    blocks, entries, width = weights.shape[1:4]
    units = micro * batch // UNIT
    dma = pltpu.SemaphoreType.DMA
    out = pl.pallas_call(
        functools.partial(
            kernel, sections, groups, units, UNIT, blocks, entries, width
        ),
        out_shape=pltpu.VMEM((micro * batch, columns), jnp.bfloat16),
        in_specs=[pl.BlockSpec(memory_space=pl.ANY)] * 4,
        out_specs=pl.BlockSpec(memory_space=pltpu.VMEM),
        scratch_shapes=[
            pltpu.SMEM((blocks, entries), jnp.int32),
            pltpu.VMEM((1, columns), jnp.float32),
            pltpu.SMEM((blocks, entries), jnp.int32),
            pltpu.VMEM((3, micro * batch, columns), jnp.bfloat16),
            pltpu.VMEM((3 * blocks, UNIT, width), jnp.bfloat16),
            pltpu.VMEM((blocks, entries, width, width), jnp.bfloat16),
            dma((2,)),
            dma((blocks,)),
            dma((units,)),
            dma((units,)),
            dma((units, 2)),
            dma((units, 2)),
            dma((units, 3)),
        ],
        compiler_params=pltpu.CompilerParams(
            collective_id=0, has_side_effects=True, vmem_limit_bytes=60 << 20
        ),
        name="sections",
    )(pattern[0], bias, inputs.reshape(micro * batch, columns), weights[0])
    return out.reshape(1, micro, batch, columns)


def solution(mesh):
    return jax.shard_map(
        functools.partial(per_device, mesh.shape["pipe"], mesh.shape["neuron"]),
        mesh=mesh,
        in_specs=(
            P(None, None, "neuron"),
            P("pipe", "neuron", None, None, None),
            P("pipe", "neuron", None),
            P("pipe", "neuron"),
        ),
        out_specs=P("pipe", None, None, "neuron"),
        check_vma=False,
    )
```
